32 devices in a mesh: image: 4 (over x, core), space: 8 (over z, y).
Axes of the slice: x: 2, y: 2, z: 4, core: 2. Of those that a mesh axis runs over, the one named last changes fastest.
Arguments:
- positions: float32 [8, 3, 2048], P('image', None, 'space'), may hold values from -6 to 6
- velocity: float32 [8, 3, 2048], P('image', None, 'space'), may hold values from -4 to 4
- start_state: float32 [3, 2048], P(None, 'space'), may hold values from -6 to 6
- end_state: float32 [3, 2048], P(None, 'space'), may hold values from -6 to 6
- neighbours: int32 [8, 16, 2048], P('image', None, 'space'), may hold values from 0 to 511, as said below
- counts: int32 [8, 2048], P('image', 'space'), may hold values from 1 to 16, as said below
- climb_index: int32 [1], replicated, may hold values from 0 to 7
- radial_a1: float32 [8, 64], replicated, may hold values from -2 to 2
- radial_b1: float32 [64, 128], replicated, may hold values from -0.75 to 0.75
- mix_first: float32 [384, 128], replicated, may hold values from -0.5 to 0.5
- read_first: float32 [128], replicated, may hold values from -0.5 to 0.5
- radial_a2: float32 [8, 64], replicated, may hold values from -2 to 2
- radial_b2: float32 [64, 128], replicated, may hold values from -0.75 to 0.75
- mix_second: float32 [384, 128], replicated, may hold values from -0.5 to 0.5
- read_second: float32 [128], replicated, may hold values from -0.5 to 0.5
Outputs:
- neb_force: float32 [8, 3, 2048], P('image', None, 'space')
- velocity_next: float32 [8, 3, 2048], P('image', None, 'space')
- position_next: float32 [8, 3, 2048], P('image', None, 'space')
- image_energy: float32 [8], P('image')
The draws below stay inside these ranges and needn't reach their ends.
Inputs may be any that keep to these rules, and one draw needn't show every extreme that they name: `neighbours`: A slab's extended atoms are, in order, the last 128 atoms of the slab below, its own 256 atoms, and the first 128 atoms of the slab above; the first and last slabs are beside each other. `counts`: atoms in the middle of the image have a higher least number of live neighbours than those at its ends.
All inputs are finite; a program needn't handle non-finite values.
Results may differ from the reference program's by a relative error of at most 0.0003.
Values sent between devices are 32-bit elements; how exact they have to be, the bound alone decides.
A program may use at most 64 MiB of HBM per device.

```python
import math
import jax
import jax.numpy as jnp
from jax import lax

CH = 128
RH = 64
NB = 8
NBR = 16
ATOMS_DEV = 256
GHOST = 128
IMAGES = 8
ATOMS = 2048


def draw_neighbours(key, part):
    extent = ATOMS_DEV + 2 * GHOST
    picked = jax.random.randint(key, (IMAGES, NBR, ATOMS), 0, extent).astype(jnp.int32)
    picked = picked.at[:, 0, 0].set(extent - 1)
    return picked.at[:, 1, 0].set(0)


def draw_counts(key, part):
    atom = jnp.arange(ATOMS).astype(jnp.int32)
    lowest = 1 + (NBR - 1) * (ATOMS - jnp.abs(2 * atom - ATOMS)) // ATOMS
    raw = jax.random.randint(jax.random.fold_in(key, 7), (IMAGES, ATOMS), 0, 1 << 20).astype(jnp.int32)
    widths = NBR - lowest + 1
    drawn = (lowest[None] + raw % widths[None]).astype(jnp.int32)
    return drawn.at[:, 0].set(1)


def block_scale(rng, shape, cuts, low, top_value):
    level = 1.0
    for axis_at, parts in cuts:
        draws = jax.random.uniform(jax.random.fold_in(jax.random.fold_in(rng, 6), axis_at), (parts,), jnp.float32, low / len(cuts), top_value / len(cuts))
        level = level * jnp.repeat(jnp.exp(draws), shape[axis_at] // parts).reshape((-1,) + (1,) * (len(shape) - 1 - axis_at))
    return level


def scatter_about(rng, dims, scale, limit, pieces=(), kind=jnp.bfloat16):
    result = scale * jax.random.normal(rng, dims, jnp.float32)
    if pieces:
        result = result * block_scale(rng, dims, pieces, -0.22, 0.18)
    return jnp.clip(result, -limit, limit).astype(kind)


def setup_inputs(seed: int = 0) -> dict:
    arg_keys = jax.random.split(jax.random.key(seed), 16)
    return {
        "positions": scatter_about(arg_keys[0], (IMAGES, 3, ATOMS), 1.0, 6.0, ((0, 4), (2, 8)), jnp.float32),
        "velocity": scatter_about(arg_keys[1], (IMAGES, 3, ATOMS), 0.5, 4.0, ((0, 4), (2, 8)), jnp.float32),
        "start_state": scatter_about(arg_keys[2], (3, ATOMS), 1.0, 6.0, ((1, 8),), jnp.float32),
        "end_state": scatter_about(arg_keys[3], (3, ATOMS), 1.0, 6.0, ((1, 8),), jnp.float32),
        "neighbours": draw_neighbours(jax.random.fold_in(arg_keys[15], 71), 0),
        "counts": draw_counts(jax.random.fold_in(arg_keys[15], 71), 0),
        "climb_index": jax.random.randint(arg_keys[6], (1,), 0, IMAGES).astype(jnp.int32),
        "radial_a1": scatter_about(arg_keys[7], (NB, RH), NB ** -0.5, 2.0, (), jnp.float32),
        "radial_b1": scatter_about(arg_keys[8], (RH, CH), RH ** -0.5, 0.75, (), jnp.float32),
        "mix_first": scatter_about(arg_keys[9], (3 * CH, CH), CH ** -0.5, 0.5, (), jnp.float32),
        "read_first": scatter_about(arg_keys[10], (CH,), CH ** -0.5, 0.5, (), jnp.float32),
        "radial_a2": scatter_about(arg_keys[11], (NB, RH), NB ** -0.5, 2.0, (), jnp.float32),
        "radial_b2": scatter_about(arg_keys[12], (RH, CH), RH ** -0.5, 0.75, (), jnp.float32),
        "mix_second": scatter_about(arg_keys[13], (3 * CH, CH), CH ** -0.5, 0.5, (), jnp.float32),
        "read_second": scatter_about(arg_keys[14], (CH,), CH ** -0.5, 0.5, (), jnp.float32),
    }


highest = lax.Precision.HIGHEST

def harmonics(unit):
    ux = unit[0]
    uy = unit[1]
    uz = unit[2]
    return jnp.stack([jnp.ones_like(ux), ux, uy, uz, ux * uy, uy * uz, ux * uz, 0.5 * (ux * ux - uy * uy), (3.0 * uz * uz - 1.0) / (2.0 * math.sqrt(3.0))])

def layer_out(center, nb_pos, live_mask, radial_a, radial_b, mixing, nb_feat):
    offset = nb_pos - center[:, None, :]
    length = jnp.sqrt(lax.optimization_barrier(jnp.sum(offset * offset, axis=0)) + 1.0)
    angular = harmonics(offset / length[None])
    centres = 0.5 * jnp.arange(radial_a.shape[0]).astype(center.dtype)
    spread = length[None] - centres[:, None, None]
    basis = jnp.exp(-spread * spread / 0.5)
    hidden = jax.nn.silu(jnp.einsum('bka,bh->hka', basis, radial_a, precision=highest))
    radial = jnp.einsum('hka,hc->cka', hidden, radial_b, precision=highest) * live_mask[None]
    if nb_feat is not None:
        radial = radial * nb_feat
    moments = jnp.einsum('cka,lka->cla', radial, angular, precision=highest) / live_mask.shape[0]
    invariants = jnp.concatenate([moments[:, 0], lax.optimization_barrier(jnp.sum(moments[:, 1:4] * moments[:, 1:4], axis=1)), lax.optimization_barrier(jnp.sum(moments[:, 4:9] * moments[:, 4:9], axis=1))], axis=0)
    return jax.nn.silu(jnp.einsum('fa,fc->ca', invariants, mixing, precision=highest))

def reference(positions, velocity, start_state, end_state, neighbours, counts, climb_index, radial_a1, radial_b1, mix_first, read_first, radial_a2, radial_b2, mix_second, read_second):

    def total_energy(image_pos, nb_idx, live_mask):
        atoms = image_pos.shape[1]
        slab = jnp.arange(atoms).astype(jnp.int32) // ATOMS_DEV
        global_nb = ((slab[None] * ATOMS_DEV + nb_idx - GHOST) % atoms).astype(jnp.int32)
        nb_pos = image_pos[:, global_nb]
        first = layer_out(image_pos, nb_pos, live_mask, radial_a1, radial_b1, mix_first, None)
        second = layer_out(image_pos, nb_pos, live_mask, radial_a2, radial_b2, mix_second, first[:, global_nb])
        return jnp.sum(read_first[:, None] * first) + jnp.sum(read_second[:, None] * second)

    def per_image(items):
        image_pos, nb_idx, live_count = items
        slots = lax.broadcasted_iota(jnp.int32, nb_idx.shape, 0)
        live_mask = (slots < live_count[None]).astype(image_pos.dtype)
        energy, grad_pos = jax.value_and_grad(total_energy)(image_pos, nb_idx, live_mask)
        return (energy, -grad_pos)
    energies, forces = lax.map(per_image, (positions, neighbours, counts))
    prev_pos = jnp.concatenate([start_state[None], positions[:-1]], axis=0)
    next_pos = jnp.concatenate([positions[1:], end_state[None]], axis=0)
    spread = next_pos - prev_pos
    ahead = next_pos - positions
    behind = positions - prev_pos
    dist_ahead = lax.optimization_barrier(jnp.sum(ahead * ahead, axis=(1, 2)))
    dist_behind = lax.optimization_barrier(jnp.sum(behind * behind, axis=(1, 2)))
    spread_sq = lax.optimization_barrier(jnp.sum(spread * spread, axis=(1, 2)))
    tangent = spread / jnp.sqrt(spread_sq + 1e-06)[:, None, None]
    along = lax.optimization_barrier(jnp.sum(forces * tangent, axis=(1, 2)))
    spring = 5.0 * (jnp.sqrt(dist_ahead) - jnp.sqrt(dist_behind))
    climbing = (jnp.arange(positions.shape[0]).astype(jnp.int32) == climb_index[0]).astype(positions.dtype)
    coef = -(1.0 + climbing) * along + (1.0 - climbing) * spring
    neb_force = forces + coef[:, None, None] * tangent
    vel_sq = jnp.sum(velocity * velocity)
    force_sq = jnp.sum(neb_force * neb_force)
    velocity_next = 0.9 * velocity + 0.1 * jnp.sqrt(vel_sq / (force_sq + 1e-06)) * neb_force + 0.1 * neb_force
    position_next = positions + 0.1 * velocity_next
    return (neb_force, velocity_next, position_next, energies / positions.shape[2])
```

```python
import functools
import math

import jax
import jax.numpy as jnp
from jax import lax
from jax.experimental import pallas as pl
from jax.experimental.pallas import tpu as pltpu
from jax.sharding import PartitionSpec as P

f32 = jnp.float32
b16 = jnp.bfloat16
ROOT3 = math.sqrt(3.0)


def nn(a, b):
    return lax.dot_general(a, b, (((1,), (0,)), ((), ())), preferred_element_type=f32)


def nt(a, b):
    return lax.dot_general(a, b, (((1,), (1,)), ((), ())), preferred_element_type=f32)


def pieces(x):
    high = x.astype(b16).astype(f32)
    return high, x - high


def rows(*parts):
    return jnp.concatenate(parts, axis=0).astype(b16)


def eye(size):
    r = lax.broadcasted_iota(jnp.int32, (size, size), 0)
    c = lax.broadcasted_iota(jnp.int32, (size, size), 1)
    return jnp.where(r == c, 1.0, 0.0).astype(b16)


def total(x):
    return jnp.sum(jnp.sum(x, axis=1, keepdims=True), axis=0, keepdims=True)


def kernel(
    n_image,
    n_space,
    pos,
    vel,
    first_end,
    last_end,
    nbr,
    cnt,
    climb,
    a1,
    b1,
    m1,
    q1,
    a2,
    b2,
    m2,
    q2,
    neb_out,
    vel_out,
    pos_out,
    en_out,
    hot,
    ext,
    nbp,
    geo,
    ang,
    dang,
    dlen,
    rad1,
    rad2,
    feat_nb,
    slope1,
    slope2,
    mom1,
    mom2,
    oslope1,
    feat,
    gfeat,
    dq,
    drow,
    gpos,
    force,
    wa_f,
    wa_b1,
    wa_b2,
    wb_f1,
    wb_b1,
    wb_f2,
    wb_b2,
    wm_f1,
    wm_b1,
    wm_f2,
    wm_b2,
    rcol,
    energy,
    ghost_pos,
    ghost_feat,
    ghost_grad,
    ghost_force,
    side_img,
    part_a,
    part_b,
    send_edge,
    recv_edge,
    send_feat,
    recv_feat,
    send_grad,
    recv_grad,
    send_force,
    recv_force,
    send_a,
    recv_a,
    send_b,
    recv_b,
):
    imgs, _, atoms = pos.shape
    ghost = atoms // 2
    span = atoms + 2 * ghost
    slots = nbr.shape[1]
    hid = a1.shape[1]
    nb = a1.shape[0]
    ch = b1.shape[1]
    me_i = lax.axis_index("image")
    me_s = lax.axis_index("space")
    low = lax.rem(me_s + n_space - 1, n_space)
    upp = lax.rem(me_s + 1, n_space)
    prv = lax.rem(me_i + n_image - 1, n_image)
    nxt = lax.rem(me_i + 1, n_image)
    mesh_id = pl.DeviceIdType.MESH

    def remote(src, dst, ss, rs, dev):
        return pltpu.make_async_remote_copy(
            src_ref=src, dst_ref=dst, send_sem=ss, recv_sem=rs, device_id=dev, device_id_type=mesh_id
        )

    barrier = pltpu.get_barrier_semaphore()
    for off in range(1, n_space):
        pl.semaphore_signal(
            barrier, inc=1, device_id=(me_i, lax.rem(me_s + off, n_space)), device_id_type=mesh_id
        )
    for off in range(1, n_image):
        pl.semaphore_signal(
            barrier, inc=1, device_id=(lax.rem(me_i + off, n_image), me_s), device_id_type=mesh_id
        )

    place = lax.broadcasted_iota(jnp.int32, (span, atoms), 0)

    def lanes(k):
        return pl.ds(pl.multiple_of(k * atoms, atoms), atoms)

    for i in range(imgs):

        def build(k, carry, i=i):
            idx = nbr[i, pl.ds(k, 1), :]
            idx = jnp.where(cnt[i : i + 1, :] > k, idx, -1)
            hot[i, :, lanes(k)] = jnp.where(place == idx, 1.0, 0.0).astype(b16)
            return carry

        if i == 0:
            lax.fori_loop(0, slots, build, 0)
            pl.semaphore_wait(barrier, n_space - 1 + n_image - 1)
            edge = [
                remote(
                    pos.at[:, :, pl.ds(0, ghost)],
                    ghost_pos.at[1],
                    send_edge.at[0],
                    recv_edge.at[0],
                    (me_i, low),
                ),
                remote(
                    pos.at[:, :, pl.ds(atoms - ghost, ghost)],
                    ghost_pos.at[0],
                    send_edge.at[1],
                    recv_edge.at[1],
                    (me_i, upp),
                ),
                remote(
                    pos.at[0], side_img.at[1], send_edge.at[2], recv_edge.at[2], (prv, me_s)
                ),
                remote(
                    pos.at[imgs - 1], side_img.at[0], send_edge.at[3], recv_edge.at[3], (nxt, me_s)
                ),
            ]
            for c in edge:
                c.start()
        else:
            lax.fori_loop(0, slots, build, 0)

    fwd_a = []
    for a, wab in ((a1, wa_b1), (a2, wa_b2)):
        hi, lo = pieces(a[...])
        fwd_a.append(nt(eye(hid), rows(hi, hi, lo, lo)))
        both = jnp.concatenate([hi, lo], axis=0)
        wab[...] = jnp.concatenate([both, both], axis=1).astype(b16)
    wa_f[...] = rows(*fwd_a)
    unit = eye(ch)
    for b, wbf, wbb in ((b1, wb_f1, wb_b1), (b2, wb_f2, wb_b2)):
        hi, lo = pieces(b[...])
        wbf[...] = nt(unit, rows(hi, hi, lo)).astype(b16)
        both = jnp.concatenate([hi, lo], axis=0)
        wbb[...] = jnp.concatenate([both, both], axis=1).astype(b16)
    for m, wmf, wmb in ((m1, wm_f1, wm_b1), (m2, wm_f2, wm_b2)):
        hi, lo = pieces(m[...])
        wmf[...] = nt(unit, rows(hi, hi, lo)).astype(b16)
        both = jnp.concatenate([hi, lo], axis=0)
        wmb[...] = jnp.concatenate([both, both], axis=1).astype(b16)
    for j, q in enumerate((q1, q2)):
        wide = jnp.broadcast_to(q[...], (atoms, ch))
        hi, rest = pieces(wide)
        mid, lo = pieces(rest)
        rcol[j] = nt(unit, hi.astype(b16)) + nt(unit, mid.astype(b16)) + nt(unit, lo.astype(b16))

    centre = 0.5 * lax.broadcasted_iota(jnp.int32, (nb, atoms), 0).astype(f32)
    cstep = 32
    lt = 128

    def moments(i, rad, scale_by, mom):
        def block(cb, carry):
            cs = pl.ds(pl.multiple_of(cb * cstep, cstep), cstep)
            for t in range(atoms // lt):
                ls = pl.ds(t * lt, lt)
                acc = [None] * 9
                for k in range(slots):
                    r = rad[i, k, cs, ls]
                    if scale_by is not None:
                        r = r * scale_by[k, cs, ls]
                    for l in range(9):
                        term = r if l == 0 else r * ang[i, l, k : k + 1, ls]
                        acc[l] = term if k == 0 else acc[l] + term
                for l in range(9):
                    mom[l, cs, ls] = acc[l] * (1.0 / slots)
            return carry

        lax.fori_loop(0, ch // cstep, block, 0)

    def mixed(mom, wmf):
        inv0 = mom[0]
        inv1 = mom[1] * mom[1] + mom[2] * mom[2] + mom[3] * mom[3]
        inv2 = (
            mom[4] * mom[4]
            + mom[5] * mom[5]
            + mom[6] * mom[6]
            + mom[7] * mom[7]
            + mom[8] * mom[8]
        )
        h0, l0 = pieces(inv0)
        h1, l1 = pieces(inv1)
        h2, l2 = pieces(inv2)
        pre = nn(wmf[...], rows(h0, h1, h2, l0, l1, l2, h0, h1, h2))
        sig = 1.0 / (1.0 + jnp.exp(-pre))
        return pre * sig, sig * (1.0 + pre * (1.0 - sig))

    def unmixed(mom, wmb, dpre):
        hi, lo = pieces(dpre)
        both = nn(wmb[...], rows(hi, lo))
        dinv = (both[: 3 * ch] + both[3 * ch :]) * (1.0 / slots)
        mom[0] = dinv[:ch]
        d1 = 2.0 * dinv[ch : 2 * ch]
        d2 = 2.0 * dinv[2 * ch :]
        for l in range(1, 9):
            mom[l] = mom[l] * (d1 if l < 4 else d2)

    def radial_back(i, k, drad, wbb, wab, slope, add):
        hi, lo = pieces(drad)
        both = nn(wbb[...], rows(hi, lo))
        dz = (both[:hid] + both[hid:]) * slope[i, k]
        zh, zl = pieces(dz)
        db = nn(wab[...], rows(zh, zl))
        gap = geo[i, 3, pl.ds(k, 1), :] - centre
        dd = jnp.sum((db[:nb] + db[nb:]) * jnp.exp(-2.0 * gap * gap) * (-4.0 * gap), axis=0, keepdims=True)
        if add:
            dd = dd + dlen[i, pl.ds(k, 1), :]
        dlen[i, pl.ds(k, 1), :] = dd

    def phase_one(i):
        ext[...] = jnp.zeros_like(ext)
        ext[0:3, pl.ds(0, ghost)] = ghost_pos[0, i]
        ext[0:3, pl.ds(ghost, atoms)] = pos[i]
        ext[0:3, pl.ds(ghost + atoms, ghost)] = ghost_pos[1, i]
        hi, rest = pieces(ext[...])
        mid, lo = pieces(rest)
        three = rows(hi, mid, lo, jnp.zeros_like(lo))

        def pick(k, carry):
            got = nn(three, hot[i, :, lanes(k)])
            got = got[0:8] + got[8:16] + got[16:24]
            for c in range(3):
                nbp[c, pl.ds(k, 1), :] = got[c : c + 1]
            return carry

        lax.fori_loop(0, slots, pick, 0)
        r = [nbp[c] - pos[i, c : c + 1, :] for c in range(3)]
        sq = r[0] * r[0] + r[1] * r[1] + r[2] * r[2] + 1.0
        length = jnp.sqrt(sq)
        inverse = 1.0 / length
        ux, uy, uz = r[0] * inverse, r[1] * inverse, r[2] * inverse
        geo[i, 0], geo[i, 1], geo[i, 2], geo[i, 3] = ux, uy, uz, length
        ang[i, 1], ang[i, 2], ang[i, 3] = ux, uy, uz
        ang[i, 4] = ux * uy
        ang[i, 5] = uy * uz
        ang[i, 6] = ux * uz
        ang[i, 7] = 0.5 * (ux * ux - uy * uy)
        ang[i, 8] = (3.0 * uz * uz - 1.0) / (2.0 * ROOT3)

        def radial(k, carry):
            gap = geo[i, 3, pl.ds(k, 1), :] - centre
            hi, lo = pieces(jnp.exp(-2.0 * gap * gap))
            z = nn(wa_f[...], rows(hi, lo, hi, lo))
            sig = 1.0 / (1.0 + jnp.exp(-z))
            h = z * sig
            slope = sig * (1.0 + z * (1.0 - sig))
            slope1[i, k] = slope[:hid]
            slope2[i, k] = slope[hid:]
            hh, hl = pieces(h)
            alive = jnp.where(cnt[i : i + 1, :] > k, 1.0, 0.0)
            rad1[i, k] = nn(wb_f1[...], rows(hh[:hid], hl[:hid], hh[:hid])) * alive
            rad2[i, k] = nn(wb_f2[...], rows(hh[hid:], hl[hid:], hh[hid:]))
            return carry

        lax.fori_loop(0, slots, radial, 0)
        moments(i, rad1, None, mom1.at[i])
        out, slope = mixed(mom1.at[i], wm_f1)
        oslope1[i] = slope
        feat[i] = out
        energy[i] = total(out * rcol[0])

    def phase_two(i):
        whole = jnp.concatenate([ghost_feat[0, i], feat[i], ghost_feat[1, i]], axis=1)
        two = rows(*pieces(whole))

        def pick(k, carry):
            got = nn(two, hot[i, :, lanes(k)])
            feat_nb[k] = got[:ch] + got[ch:]
            return carry

        lax.fori_loop(0, slots, pick, 0)
        moments(i, rad2, feat_nb, mom2)
        out, slope = mixed(mom2, wm_f2)
        energy[i] = energy[i] + total(out * rcol[1])
        unmixed(mom2, wm_b2, rcol[1] * slope)

        def back(k, carry):
            row = [None] + [ang[i, l, pl.ds(k, 1), :] for l in range(1, 9)]
            sums = []
            for t in range(atoms // lt):
                ls = pl.ds(t * lt, lt)
                ys = [None] + [
                    jnp.broadcast_to(row[l][:, t * lt : (t + 1) * lt], (8, lt)) for l in range(1, 9)
                ]
                dy = [None] * 9
                for c in range(ch // 8):
                    cs = pl.ds(c * 8, 8)
                    raw = rad2[i, k, cs, ls]
                    q = feat_nb[k, cs, ls]
                    full = raw * q
                    drf = mom2[0, cs, ls]
                    for l in range(1, 9):
                        g = mom2[l, cs, ls]
                        drf = drf + g * ys[l]
                        dy[l] = g * full if c == 0 else dy[l] + g * full
                    rad2[i, k, cs, ls] = drf * q
                    feat_nb[k, cs, ls] = drf * raw
                sums.append([jnp.sum(dy[l], axis=0, keepdims=True) for l in range(1, 9)])
            for l in range(1, 9):
                dang[i, l, pl.ds(k, 1), :] = jnp.concatenate([s[l - 1] for s in sums], axis=1)
            dq[:, lanes(k)] = rows(*pieces(feat_nb[k]))
            radial_back(i, k, rad2[i, k], wb_b2, wa_b2, slope2, False)
            return carry

        lax.fori_loop(0, slots, back, 0)
        both = nt(dq[...], hot[i])
        gfeat[i] = both[:ch] + both[ch:]

    def phase_three(i):
        own = gfeat[i, :, pl.ds(ghost, atoms)]
        back_in = jnp.concatenate([ghost_grad[0, i], ghost_grad[1, i]], axis=1)
        unmixed(mom1.at[i], wm_b1, (own + back_in + rcol[0]) * oslope1[i])

        def back(k, carry):
            row = [None] + [ang[i, l, pl.ds(k, 1), :] for l in range(1, 9)]
            sums = []
            for t in range(atoms // lt):
                ls = pl.ds(t * lt, lt)
                ys = [None] + [
                    jnp.broadcast_to(row[l][:, t * lt : (t + 1) * lt], (8, lt)) for l in range(1, 9)
                ]
                alive = jnp.broadcast_to(jnp.where(cnt[i : i + 1, ls] > k, 1.0, 0.0), (8, lt))
                dy = [None] * 9
                for c in range(ch // 8):
                    cs = pl.ds(c * 8, 8)
                    full = rad1[i, k, cs, ls]
                    drf = mom1[i, 0, cs, ls]
                    for l in range(1, 9):
                        g = mom1[i, l, cs, ls]
                        drf = drf + g * ys[l]
                        dy[l] = g * full if c == 0 else dy[l] + g * full
                    rad1[i, k, cs, ls] = drf * alive
                sums.append([jnp.sum(dy[l], axis=0, keepdims=True) for l in range(1, 9)])
            for l in range(1, 9):
                dang[i, l, pl.ds(k, 1), :] = dang[i, l, pl.ds(k, 1), :] + jnp.concatenate(
                    [s[l - 1] for s in sums], axis=1
                )
            radial_back(i, k, rad1[i, k], wb_b1, wa_b1, slope1, True)
            return carry

        lax.fori_loop(0, slots, back, 0)
        ux, uy, uz, length = geo[i, 0], geo[i, 1], geo[i, 2], geo[i, 3]
        inverse = 1.0 / length
        y = [None] + [dang[i, l] for l in range(1, 9)]
        du = [
            y[1] + uy * y[4] + uz * y[6] + ux * y[7],
            y[2] + ux * y[4] + uz * y[5] - uy * y[7],
            y[3] + uy * y[5] + ux * y[6] + ROOT3 * uz * y[8],
        ]
        lean = dlen[i] - (du[0] * ux + du[1] * uy + du[2] * uz) * inverse
        drow[...] = jnp.zeros_like(drow)
        for c, u in enumerate((ux, uy, uz)):
            dr = du[c] * inverse + u * lean
            for k in range(slots):
                drow[c : c + 1, k * atoms : (k + 1) * atoms] = dr[k : k + 1]
            force[i, c : c + 1, :] = jnp.sum(dr, axis=0, keepdims=True)
        both = nt(rows(*pieces(drow[...])), hot[i])
        gpos[i] = both[:8] + both[8:]

    def swap(i, src, head, tail, dst_upper, dst_lower, ss, rs):
        pair = [
            remote(src.at[i, :, head], dst_upper.at[i], ss.at[i, 0], rs.at[i, 0], (me_i, low)),
            remote(src.at[i, :, tail], dst_lower.at[i], ss.at[i, 1], rs.at[i, 1], (me_i, upp)),
        ]
        for c in pair:
            c.start()
        return pair

    own_head, own_tail = pl.ds(0, ghost), pl.ds(atoms - ghost, ghost)
    ext_head, ext_tail = pl.ds(0, ghost), pl.ds(ghost + atoms, ghost)
    for c in edge:
        c.wait()
    sent = []
    for i in range(imgs):
        phase_one(i)
        sent.append(
            swap(
                i, feat, own_head, own_tail, ghost_feat.at[1], ghost_feat.at[0], send_feat, recv_feat
            )
        )
    back_sent = []
    for i in range(imgs):
        for c in sent[i]:
            c.wait()
        phase_two(i)
        back_sent.append(
            swap(
                i, gfeat, ext_head, ext_tail, ghost_grad.at[1], ghost_grad.at[0], send_grad, recv_grad
            )
        )
    force_sent = []
    for i in range(imgs):
        for c in back_sent[i]:
            c.wait()
        phase_three(i)
        force_sent.append(
            swap(
                i, gpos, ext_head, ext_tail, ghost_force.at[1], ghost_force.at[0], send_force, recv_force
            )
        )

    lane = lax.broadcasted_iota(jnp.int32, (8, 128), 1)
    line = lax.broadcasted_iota(jnp.int32, (8, 128), 0)
    spreads = []
    vv = jnp.zeros((1, 1), f32)
    block = jnp.zeros((8, 128), f32)
    for i in range(imgs):
        here = pos[i]
        if i == 0:
            before = jnp.where(me_i == 0, first_end[...], side_img[0])
        else:
            before = pos[i - 1]
        if i == imgs - 1:
            after = jnp.where(me_i == n_image - 1, last_end[...], side_img[1])
        else:
            after = pos[i + 1]
        spread = after - before
        spreads.append(spread)
        ahead = after - here
        behind = here - before
        vv = vv + total(vel[i] * vel[i])
        for c in force_sent[i]:
            c.wait()
        back_in = jnp.concatenate([ghost_force[0, i], ghost_force[1, i]], axis=1)
        f = force[i] - gpos[i, 0:3, pl.ds(ghost, atoms)] - back_in[0:3]
        force[i] = f
        values = (
            total(ahead * ahead),
            total(behind * behind),
            total(spread * spread),
            energy[i],
            total(f * spread),
            total(f * f),
        )
        for j, v in enumerate(values):
            block = jnp.where((line == i) & (lane == j), v, block)
    block = jnp.where((line == imgs) & (lane == 0), vv, block)

    def everywhere(block, part, ss, rs, count, mine, device):
        part[mine] = block
        out = []
        for off in range(1, count):
            peer = lax.rem(mine + off, count)
            c = remote(part.at[mine], part.at[mine], ss.at[off], rs.at[mine], device(peer))
            c.start()
            out.append(c)
        for off in range(1, count):
            peer = lax.rem(mine + off, count)
            remote(
                part.at[mine], part.at[peer], ss.at[off], rs.at[peer], device(peer)
            ).wait_recv()
        for c in out:
            c.wait_send()
        summed = part[0]
        for j in range(1, count):
            summed = summed + part[j]
        return summed

    summed = everywhere(block, part_a, send_a, recv_a, n_space, me_s, lambda p: (me_i, p))
    coefs = []
    ff = jnp.zeros((1, 1), f32)
    for i in range(imgs):
        sa, sb, st, en, fd, fs = [summed[i : i + 1, j : j + 1] for j in range(6)]
        norm = jnp.sqrt(st + 1e-06)
        along = fd / norm
        spring = 5.0 * (jnp.sqrt(sa) - jnp.sqrt(sb))
        climbing = jnp.where(me_i * imgs + i == climb[0], 1.0, 0.0)
        coef = (-(1.0 + climbing) * along + (1.0 - climbing) * spring) / norm
        coefs.append(coef)
        ff = ff + jnp.maximum(fs + 2.0 * coef * fd + coef * coef * st, 0.0)
        en_out[i : i + 1, :] = jnp.broadcast_to(en / (atoms * n_space), (1, 128))
    block = jnp.where(lane == 0, summed[imgs : imgs + 1, 0:1], 0.0)
    block = jnp.where(lane == 1, ff, block)
    summed = everywhere(block, part_b, send_b, recv_b, n_image, me_i, lambda p: (p, me_s))
    ratio = 0.1 * jnp.sqrt(summed[0:1, 0:1] / (summed[0:1, 1:2] + 1e-06)) + 0.1
    for i in range(imgs):
        neb = force[i] + coefs[i] * spreads[i]
        moved = 0.9 * vel[i] + ratio * neb
        neb_out[i] = neb
        vel_out[i] = moved
        pos_out[i] = pos[i] + 0.1 * moved


def local(n_image, n_space, *args):
    pos, nbr, a1, b1 = args[0], args[4], args[7], args[8]
    imgs, _, atoms = pos.shape
    slots = nbr.shape[1]
    nb, hid = a1.shape
    ch = b1.shape[1]
    ghost = atoms // 2
    span = atoms + 2 * ghost
    edges = slots * atoms
    args = list(args)
    for j in (10, 14):
        args[j] = args[j].reshape(1, -1)
    vm = pltpu.VMEM
    dma = pltpu.SemaphoreType.DMA
    scratch = [
        vm((imgs, span, edges), b16),
        vm((8, span), f32),
        vm((3, slots, atoms), f32),
        vm((imgs, 4, slots, atoms), f32),
        vm((imgs, 9, slots, atoms), f32),
        vm((imgs, 9, slots, atoms), f32),
        vm((imgs, slots, atoms), f32),
        vm((imgs, slots, ch, atoms), f32),
        vm((imgs, slots, ch, atoms), f32),
        vm((slots, ch, atoms), f32),
        vm((imgs, slots, hid, atoms), f32),
        vm((imgs, slots, hid, atoms), f32),
        vm((imgs, 9, ch, atoms), f32),
        vm((9, ch, atoms), f32),
        vm((imgs, ch, atoms), f32),
        vm((imgs, ch, atoms), f32),
        vm((imgs, ch, span), f32),
        vm((2 * ch, edges), b16),
        vm((8, edges), f32),
        vm((imgs, 8, span), f32),
        vm((imgs, 3, atoms), f32),
        vm((2 * hid, 4 * nb), b16),
        vm((2 * nb, 2 * hid), b16),
        vm((2 * nb, 2 * hid), b16),
        vm((ch, 3 * hid), b16),
        vm((2 * hid, 2 * ch), b16),
        vm((ch, 3 * hid), b16),
        vm((2 * hid, 2 * ch), b16),
        vm((ch, 9 * ch), b16),
        vm((6 * ch, 2 * ch), b16),
        vm((ch, 9 * ch), b16),
        vm((6 * ch, 2 * ch), b16),
        vm((2, ch, atoms), f32),
        vm((imgs, 1, 1), f32),
        vm((2, imgs, 3, ghost), f32),
        vm((2, imgs, ch, ghost), f32),
        vm((2, imgs, ch, ghost), f32),
        vm((2, imgs, 8, ghost), f32),
        vm((2, 3, atoms), f32),
        vm((n_space, 8, 128), f32),
        vm((n_image, 8, 128), f32),
        dma((4,)),
        dma((4,)),
        dma((imgs, 2)),
        dma((imgs, 2)),
        dma((imgs, 2)),
        dma((imgs, 2)),
        dma((imgs, 2)),
        dma((imgs, 2)),
        dma((n_space,)),
        dma((n_space,)),
        dma((n_image,)),
        dma((n_image,)),
    ]
    in_specs = [pl.BlockSpec(memory_space=pltpu.VMEM)] * len(args)
    in_specs[6] = pl.BlockSpec(memory_space=pltpu.SMEM)
    state = jax.ShapeDtypeStruct(pos.shape, f32)
    neb, vel, new, en = pl.pallas_call(
        functools.partial(kernel, n_image, n_space),
        out_shape=[state, state, state, jax.ShapeDtypeStruct((imgs, 128), f32)],
        in_specs=in_specs,
        out_specs=[pl.BlockSpec(memory_space=pltpu.VMEM)] * 4,
        scratch_shapes=scratch,
        compiler_params=pltpu.CompilerParams(
            collective_id=0, has_side_effects=True, vmem_limit_bytes=56 * 1024 * 1024
        ),
    )(*args)
    return neb, vel, new, en[:, 0]


def solution(mesh):
    state = P("image", None, "space")
    end = P(None, "space")
    in_specs = (state, state, end, end, state, P("image", "space")) + (P(),) * 9
    out_specs = (state, state, state, P("image"))
    body = functools.partial(local, mesh.shape["image"], mesh.shape["space"])
    return jax.shard_map(body, mesh=mesh, in_specs=in_specs, out_specs=out_specs, check_vma=False)
```

```python
import functools
import math

import jax
import jax.numpy as jnp
from jax import lax
from jax.experimental import pallas as pl
from jax.experimental.pallas import tpu as pltpu
from jax.sharding import PartitionSpec as P

f32 = jnp.float32
b16 = jnp.bfloat16
ROOT3 = math.sqrt(3.0)


def nn(a, b):
    return lax.dot_general(a, b, (((1,), (0,)), ((), ())), preferred_element_type=f32)


def nt(a, b):
    return lax.dot_general(a, b, (((1,), (1,)), ((), ())), preferred_element_type=f32)


def pieces(x):
    high = x.astype(b16).astype(f32)
    return high, x - high


def rows(*parts):
    return jnp.concatenate(parts, axis=0).astype(b16)


def eye(size):
    r = lax.broadcasted_iota(jnp.int32, (size, size), 0)
    c = lax.broadcasted_iota(jnp.int32, (size, size), 1)
    return jnp.where(r == c, 1.0, 0.0).astype(b16)


def total(x):
    return jnp.sum(jnp.sum(x, axis=1, keepdims=True), axis=0, keepdims=True)


def kernel(
    n_image,
    n_space,
    pos_in,
    vel_in,
    first_end,
    last_end,
    nbr,
    cnt,
    climb,
    a1,
    b1,
    m1,
    q1,
    a2,
    b2,
    m2,
    q2,
    neb_out,
    vel_out,
    pos_out,
    en_out,
    pos,
    vel,
    hot,
    ext,
    nbp,
    geo,
    ang,
    dang,
    dlen,
    rad1,
    rad2,
    feat_nb,
    slope1,
    slope2,
    mom1,
    mom2,
    oslope1,
    feat,
    gfeat,
    dq,
    drow,
    gpos,
    force,
    wa_f,
    wa_b1,
    wa_b2,
    wb_f1,
    wb_b1,
    wb_f2,
    wb_b2,
    wm_f1,
    wm_b1,
    wm_f2,
    wm_b2,
    rcol,
    energy,
    ghost_pos,
    ghost_feat,
    ghost_grad,
    ghost_force,
    side_img,
    part_a,
    part_b,
    send_edge,
    recv_edge,
    send_feat,
    recv_feat,
    send_grad,
    recv_grad,
    send_force,
    recv_force,
    send_a,
    recv_a,
    send_b,
    recv_b,
):
    _, imgs, atoms = pos_in.shape
    ghost = atoms // 2
    span = atoms + 2 * ghost
    slots = nbr.shape[1]
    hid = a1.shape[1]
    nb = a1.shape[0]
    ch = b1.shape[1]
    me_i = lax.axis_index("image")
    me_s = lax.axis_index("space")
    low = lax.rem(me_s + n_space - 1, n_space)
    upp = lax.rem(me_s + 1, n_space)
    prv = lax.rem(me_i + n_image - 1, n_image)
    nxt = lax.rem(me_i + 1, n_image)
    mesh_id = pl.DeviceIdType.MESH

    def remote(src, dst, ss, rs, dev):
        return pltpu.make_async_remote_copy(
            src_ref=src, dst_ref=dst, send_sem=ss, recv_sem=rs, device_id=dev, device_id_type=mesh_id
        )

    barrier = pltpu.get_barrier_semaphore()
    for off in range(1, n_space):
        pl.semaphore_signal(
            barrier, inc=1, device_id=(me_i, lax.rem(me_s + off, n_space)), device_id_type=mesh_id
        )
    for off in range(1, n_image):
        pl.semaphore_signal(
            barrier, inc=1, device_id=(lax.rem(me_i + off, n_image), me_s), device_id_type=mesh_id
        )

    for i in range(imgs):
        for c in range(3):
            pos[i, c : c + 1, :] = pos_in[c, i : i + 1, :]
            vel[i, c : c + 1, :] = vel_in[c, i : i + 1, :]

    place = lax.broadcasted_iota(jnp.int32, (span, atoms), 0)

    def lanes(k):
        return pl.ds(pl.multiple_of(k * atoms, atoms), atoms)

    for i in range(imgs):

        def build(k, carry, i=i):
            idx = nbr[i, pl.ds(k, 1), :]
            idx = jnp.where(cnt[i : i + 1, :] > k, idx, -1)
            hot[i, :, lanes(k)] = jnp.where(place == idx, 1.0, 0.0).astype(b16)
            return carry

        if i == 0:
            lax.fori_loop(0, slots, build, 0)
            pl.semaphore_wait(barrier, n_space - 1 + n_image - 1)
            edge = [
                remote(
                    pos.at[:, :, pl.ds(0, ghost)],
                    ghost_pos.at[1],
                    send_edge.at[0],
                    recv_edge.at[0],
                    (me_i, low),
                ),
                remote(
                    pos.at[:, :, pl.ds(atoms - ghost, ghost)],
                    ghost_pos.at[0],
                    send_edge.at[1],
                    recv_edge.at[1],
                    (me_i, upp),
                ),
                remote(
                    pos.at[0], side_img.at[1], send_edge.at[2], recv_edge.at[2], (prv, me_s)
                ),
                remote(
                    pos.at[imgs - 1], side_img.at[0], send_edge.at[3], recv_edge.at[3], (nxt, me_s)
                ),
            ]
            for c in edge:
                c.start()
        else:
            lax.fori_loop(0, slots, build, 0)

    fwd_a = []
    for a, wab in ((a1, wa_b1), (a2, wa_b2)):
        hi, lo = pieces(a[...])
        fwd_a.append(nt(eye(hid), rows(hi, hi, lo, lo)))
        both = jnp.concatenate([hi, lo], axis=0)
        wab[...] = jnp.concatenate([both, both], axis=1).astype(b16)
    wa_f[...] = rows(*fwd_a)
    unit = eye(ch)
    for b, wbf, wbb in ((b1, wb_f1, wb_b1), (b2, wb_f2, wb_b2)):
        hi, lo = pieces(b[...])
        wbf[...] = nt(unit, rows(hi, hi, lo)).astype(b16)
        both = jnp.concatenate([hi, lo], axis=0)
        wbb[...] = jnp.concatenate([both, both], axis=1).astype(b16)
    for m, wmf, wmb in ((m1, wm_f1, wm_b1), (m2, wm_f2, wm_b2)):
        hi, lo = pieces(m[...])
        wmf[...] = nt(unit, rows(hi, hi, lo)).astype(b16)
        both = jnp.concatenate([hi, lo], axis=0)
        wmb[...] = jnp.concatenate([both, both], axis=1).astype(b16)
    for j, q in enumerate((q1, q2)):
        wide = jnp.broadcast_to(q[...], (atoms, ch))
        hi, rest = pieces(wide)
        mid, lo = pieces(rest)
        rcol[j] = nt(unit, hi.astype(b16)) + nt(unit, mid.astype(b16)) + nt(unit, lo.astype(b16))

    group = 4 if slots % 4 == 0 else 1
    pair = 2 if slots % 2 == 0 else 1
    centre = 0.5 * lax.broadcasted_iota(jnp.int32, (nb, group * atoms), 0).astype(f32)

    def wide(parts):
        return jnp.concatenate(parts, axis=1)

    cstep = 32
    lt = 128

    def moments(i, rad, scale_by, mom):
        def block(cb, carry):
            cs = pl.ds(pl.multiple_of(cb * cstep, cstep), cstep)
            for t in range(atoms // lt):
                ls = pl.ds(t * lt, lt)
                acc = [None] * 9
                for k in range(slots):
                    r = rad[i, k, cs, ls]
                    if scale_by is not None:
                        r = r * scale_by[k, cs, ls]
                    for l in range(9):
                        term = r if l == 0 else r * ang[i, l, k : k + 1, ls]
                        acc[l] = term if k == 0 else acc[l] + term
                for l in range(9):
                    mom[l, cs, ls] = acc[l] * (1.0 / slots)
            return carry

        lax.fori_loop(0, ch // cstep, block, 0)

    def mixed(mom, wmf):
        inv0 = mom[0]
        inv1 = mom[1] * mom[1] + mom[2] * mom[2] + mom[3] * mom[3]
        inv2 = (
            mom[4] * mom[4]
            + mom[5] * mom[5]
            + mom[6] * mom[6]
            + mom[7] * mom[7]
            + mom[8] * mom[8]
        )
        h0, l0 = pieces(inv0)
        h1, l1 = pieces(inv1)
        h2, l2 = pieces(inv2)
        pre = nn(wmf[...], rows(h0, h1, h2, l0, l1, l2, h0, h1, h2))
        sig = 1.0 / (1.0 + jnp.exp(-pre))
        return pre * sig, sig * (1.0 + pre * (1.0 - sig))

    def unmixed(mom, wmb, dpre):
        hi, lo = pieces(dpre)
        both = nn(wmb[...], rows(hi, lo))
        dinv = (both[: 3 * ch] + both[3 * ch :]) * (1.0 / slots)
        mom[0] = dinv[:ch]
        d1 = 2.0 * dinv[ch : 2 * ch]
        d2 = 2.0 * dinv[2 * ch :]
        for l in range(1, 9):
            mom[l] = mom[l] * (d1 if l < 4 else d2)

    def radial_back(i, drad, wbb, wab, slope, add):
        def step(s, carry):
            ks = [s * group + j for j in range(group)]
            hi, lo = pieces(wide([drad[i, k] for k in ks]))
            both = nn(wbb[...], rows(hi, lo))
            dz = (both[:hid] + both[hid:]) * wide([slope[i, k] for k in ks])
            zh, zl = pieces(dz)
            db = nn(wab[...], rows(zh, zl))
            gap = wide([geo[i, 3, pl.ds(k, 1), :] for k in ks]) - centre
            db = (db[:nb] + db[nb:]) * jnp.exp(-2.0 * gap * gap) * (-4.0 * gap)
            dd = jnp.sum(db, axis=0, keepdims=True)
            if add:
                dd = dd + wide([dlen[i, pl.ds(k, 1), :] for k in ks])
            for j, k in enumerate(ks):
                dlen[i, pl.ds(k, 1), :] = dd[:, j * atoms : (j + 1) * atoms]
            return carry

        lax.fori_loop(0, slots // group, step, 0)

    def phase_one(i):
        ext[...] = jnp.zeros_like(ext)
        ext[0:3, pl.ds(0, ghost)] = ghost_pos[0, i]
        ext[0:3, pl.ds(ghost, atoms)] = pos[i]
        ext[0:3, pl.ds(ghost + atoms, ghost)] = ghost_pos[1, i]
        hi, rest = pieces(ext[...])
        mid, lo = pieces(rest)
        three = rows(hi, mid, lo, jnp.zeros_like(lo))

        got = nn(three, hot[i])
        got = got[0:8] + got[8:16] + got[16:24]
        for k in range(slots):
            for c in range(3):
                nbp[c, k : k + 1, :] = got[c : c + 1, k * atoms : (k + 1) * atoms]
        r = [nbp[c] - pos[i, c : c + 1, :] for c in range(3)]
        sq = r[0] * r[0] + r[1] * r[1] + r[2] * r[2] + 1.0
        length = jnp.sqrt(sq)
        inverse = 1.0 / length
        ux, uy, uz = r[0] * inverse, r[1] * inverse, r[2] * inverse
        geo[i, 0], geo[i, 1], geo[i, 2], geo[i, 3] = ux, uy, uz, length
        ang[i, 1], ang[i, 2], ang[i, 3] = ux, uy, uz
        ang[i, 4] = ux * uy
        ang[i, 5] = uy * uz
        ang[i, 6] = ux * uz
        ang[i, 7] = 0.5 * (ux * ux - uy * uy)
        ang[i, 8] = (3.0 * uz * uz - 1.0) / (2.0 * ROOT3)

        def radial(s, carry):
            ks = [s * group + j for j in range(group)]
            gap = wide([geo[i, 3, pl.ds(k, 1), :] for k in ks]) - centre
            hi, lo = pieces(jnp.exp(-2.0 * gap * gap))
            z = nn(wa_f[...], rows(hi, lo, hi, lo))
            sig = 1.0 / (1.0 + jnp.exp(-z))
            h = z * sig
            slope = sig * (1.0 + z * (1.0 - sig))
            hh, hl = pieces(h)
            alive = wide([jnp.where(cnt[i : i + 1, :] > k, 1.0, 0.0) for k in ks])
            r1 = nn(wb_f1[...], rows(hh[:hid], hl[:hid], hh[:hid])) * alive
            r2 = nn(wb_f2[...], rows(hh[hid:], hl[hid:], hh[hid:]))
            for j, k in enumerate(ks):
                at = slice(j * atoms, (j + 1) * atoms)
                slope1[i, k] = slope[:hid, at]
                slope2[i, k] = slope[hid:, at]
                rad1[i, k] = r1[:, at]
                rad2[i, k] = r2[:, at]
            return carry

        lax.fori_loop(0, slots // group, radial, 0)
        moments(i, rad1, None, mom1.at[i])
        out, slope = mixed(mom1.at[i], wm_f1)
        oslope1[i] = slope
        feat[i] = out
        energy[i] = total(out * rcol[0])

    def phase_two(i):
        whole = jnp.concatenate([ghost_feat[0, i], feat[i], ghost_feat[1, i]], axis=1)
        two = rows(*pieces(whole))

        def pick(s, carry):
            cols = pl.ds(pl.multiple_of(s * group * atoms, group * atoms), group * atoms)
            got = nn(two, hot[i, :, cols])
            got = got[:ch] + got[ch:]
            for j in range(group):
                feat_nb[s * group + j] = got[:, j * atoms : (j + 1) * atoms]
            return carry

        lax.fori_loop(0, slots // group, pick, 0)
        moments(i, rad2, feat_nb, mom2)
        out, slope = mixed(mom2, wm_f2)
        energy[i] = energy[i] + total(out * rcol[1])
        unmixed(mom2, wm_b2, rcol[1] * slope)

        def back(s, carry):
            ks = [s * pair + j for j in range(pair)]
            row = [[None] + [ang[i, l, pl.ds(k, 1), :] for l in range(1, 9)] for k in ks]
            sums = [[] for k in ks]
            for t in range(atoms // lt):
                ls = pl.ds(t * lt, lt)
                ys = [
                    [None] + [jnp.broadcast_to(r[:, t * lt : (t + 1) * lt], (8, lt)) for r in w[1:]]
                    for w in row
                ]
                dy = [[None] * 9 for k in ks]
                for c in range(ch // 8):
                    cs = pl.ds(c * 8, 8)
                    raw = [rad2[i, k, cs, ls] for k in ks]
                    q = [feat_nb[k, cs, ls] for k in ks]
                    full = [x * y for x, y in zip(raw, q)]
                    drf = [mom2[0, cs, ls]] * pair
                    for l in range(1, 9):
                        g = mom2[l, cs, ls]
                        for j in range(pair):
                            drf[j] = drf[j] + g * ys[j][l]
                            term = g * full[j]
                            dy[j][l] = term if c == 0 else dy[j][l] + term
                    for j, k in enumerate(ks):
                        rad2[i, k, cs, ls] = drf[j] * q[j]
                        feat_nb[k, cs, ls] = drf[j] * raw[j]
                for j in range(pair):
                    sums[j].append([jnp.sum(x, axis=0, keepdims=True) for x in dy[j][1:]])
            for j, k in enumerate(ks):
                for l in range(1, 9):
                    dang[i, l, pl.ds(k, 1), :] = wide([x[l - 1] for x in sums[j]])
                dq[:, lanes(k)] = rows(*pieces(feat_nb[k]))
            return carry

        lax.fori_loop(0, slots // pair, back, 0)
        both = nt(dq[...], hot[i])
        gfeat[i] = both[:ch] + both[ch:]

    def phase_two_rest(i):
        radial_back(i, rad2, wb_b2, wa_b2, slope2, False)

    def phase_three(i):
        own = gfeat[i, :, pl.ds(ghost, atoms)]
        back_in = jnp.concatenate([ghost_grad[0, i], ghost_grad[1, i]], axis=1)
        unmixed(mom1.at[i], wm_b1, (own + back_in + rcol[0]) * oslope1[i])

        def back(s, carry):
            ks = [s * pair + j for j in range(pair)]
            row = [[None] + [ang[i, l, pl.ds(k, 1), :] for l in range(1, 9)] for k in ks]
            old = [[None] + [dang[i, l, pl.ds(k, 1), :] for l in range(1, 9)] for k in ks]
            sums = [[] for k in ks]
            for t in range(atoms // lt):
                ls = pl.ds(t * lt, lt)
                ys = [
                    [None] + [jnp.broadcast_to(r[:, t * lt : (t + 1) * lt], (8, lt)) for r in w[1:]]
                    for w in row
                ]
                alive = [
                    jnp.broadcast_to(jnp.where(cnt[i : i + 1, ls] > k, 1.0, 0.0), (8, lt)) for k in ks
                ]
                dy = [[None] * 9 for k in ks]
                for c in range(ch // 8):
                    cs = pl.ds(c * 8, 8)
                    full = [rad1[i, k, cs, ls] for k in ks]
                    drf = [mom1[i, 0, cs, ls]] * pair
                    for l in range(1, 9):
                        g = mom1[i, l, cs, ls]
                        for j in range(pair):
                            drf[j] = drf[j] + g * ys[j][l]
                            term = g * full[j]
                            dy[j][l] = term if c == 0 else dy[j][l] + term
                    for j, k in enumerate(ks):
                        rad1[i, k, cs, ls] = drf[j] * alive[j]
                for j in range(pair):
                    sums[j].append([jnp.sum(x, axis=0, keepdims=True) for x in dy[j][1:]])
            for j, k in enumerate(ks):
                for l in range(1, 9):
                    dang[i, l, pl.ds(k, 1), :] = old[j][l] + wide([x[l - 1] for x in sums[j]])
            return carry

        lax.fori_loop(0, slots // pair, back, 0)
        radial_back(i, rad1, wb_b1, wa_b1, slope1, True)
        ux, uy, uz, length = geo[i, 0], geo[i, 1], geo[i, 2], geo[i, 3]
        inverse = 1.0 / length
        y = [None] + [dang[i, l] for l in range(1, 9)]
        du = [
            y[1] + uy * y[4] + uz * y[6] + ux * y[7],
            y[2] + ux * y[4] + uz * y[5] - uy * y[7],
            y[3] + uy * y[5] + ux * y[6] + ROOT3 * uz * y[8],
        ]
        lean = dlen[i] - (du[0] * ux + du[1] * uy + du[2] * uz) * inverse
        drow[...] = jnp.zeros_like(drow)
        for c, u in enumerate((ux, uy, uz)):
            dr = du[c] * inverse + u * lean
            for k in range(slots):
                drow[c : c + 1, k * atoms : (k + 1) * atoms] = dr[k : k + 1]
            force[i, c : c + 1, :] = jnp.sum(dr, axis=0, keepdims=True)
        both = nt(rows(*pieces(drow[...])), hot[i])
        gpos[i] = both[:8] + both[8:]

    def swap(i, src, head, tail, dst_upper, dst_lower, ss, rs):
        both = [
            remote(src.at[i, :, head], dst_upper.at[i], ss.at[i, 0], rs.at[i, 0], (me_i, low)),
            remote(src.at[i, :, tail], dst_lower.at[i], ss.at[i, 1], rs.at[i, 1], (me_i, upp)),
        ]
        for c in both:
            c.start()
        return both

    own_head, own_tail = pl.ds(0, ghost), pl.ds(atoms - ghost, ghost)
    ext_head, ext_tail = pl.ds(0, ghost), pl.ds(ghost + atoms, ghost)
    for c in edge:
        c.wait()
    sent = []
    for i in range(imgs):
        phase_one(i)
        sent.append(
            swap(
                i, feat, own_head, own_tail, ghost_feat.at[1], ghost_feat.at[0], send_feat, recv_feat
            )
        )
    back_sent = []
    for i in range(imgs):
        for c in sent[i]:
            c.wait()
        phase_two(i)
        back_sent.append(
            swap(
                i, gfeat, ext_head, ext_tail, ghost_grad.at[1], ghost_grad.at[0], send_grad, recv_grad
            )
        )
        phase_two_rest(i)
    force_sent = []
    for i in range(imgs):
        for c in back_sent[i]:
            c.wait()
        phase_three(i)
        force_sent.append(
            swap(
                i, gpos, ext_head, ext_tail, ghost_force.at[1], ghost_force.at[0], send_force, recv_force
            )
        )

    lane = lax.broadcasted_iota(jnp.int32, (8, 128), 1)
    line = lax.broadcasted_iota(jnp.int32, (8, 128), 0)
    spreads = []
    vv = jnp.zeros((1, 1), f32)
    block = jnp.zeros((8, 128), f32)
    for i in range(imgs):
        here = pos[i]
        if i == 0:
            before = jnp.where(me_i == 0, first_end[...], side_img[0])
        else:
            before = pos[i - 1]
        if i == imgs - 1:
            after = jnp.where(me_i == n_image - 1, last_end[...], side_img[1])
        else:
            after = pos[i + 1]
        spread = after - before
        spreads.append(spread)
        ahead = after - here
        behind = here - before
        vv = vv + total(vel[i] * vel[i])
        for c in force_sent[i]:
            c.wait()
        back_in = jnp.concatenate([ghost_force[0, i], ghost_force[1, i]], axis=1)
        f = force[i] - gpos[i, 0:3, pl.ds(ghost, atoms)] - back_in[0:3]
        force[i] = f
        values = (
            total(ahead * ahead),
            total(behind * behind),
            total(spread * spread),
            energy[i],
            total(f * spread),
            total(f * f),
        )
        for j, v in enumerate(values):
            block = jnp.where((line == i) & (lane == j), v, block)
    block = jnp.where((line == imgs) & (lane == 0), vv, block)

    def everywhere(block, part, ss, rs, count, mine, device):
        part[mine] = block
        out = []
        for off in range(1, count):
            peer = lax.rem(mine + off, count)
            c = remote(part.at[mine], part.at[mine], ss.at[off], rs.at[mine], device(peer))
            c.start()
            out.append(c)
        for off in range(1, count):
            peer = lax.rem(mine + off, count)
            remote(
                part.at[mine], part.at[peer], ss.at[off], rs.at[peer], device(peer)
            ).wait_recv()
        for c in out:
            c.wait_send()
        summed = part[0]
        for j in range(1, count):
            summed = summed + part[j]
        return summed

    summed = everywhere(block, part_a, send_a, recv_a, n_space, me_s, lambda p: (me_i, p))
    coefs = []
    ff = jnp.zeros((1, 1), f32)
    for i in range(imgs):
        sa, sb, st, fd, fs = [summed[i : i + 1, j : j + 1] for j in (0, 1, 2, 4, 5)]
        norm = jnp.sqrt(st + 1e-06)
        along = fd / norm
        spring = 5.0 * (jnp.sqrt(sa) - jnp.sqrt(sb))
        climbing = jnp.where(me_i * imgs + i == climb[0], 1.0, 0.0)
        coef = (-(1.0 + climbing) * along + (1.0 - climbing) * spring) / norm
        coefs.append(coef)
        ff = ff + jnp.maximum(fs + 2.0 * coef * fd + coef * coef * st, 0.0)
        mine = jnp.where((line == i) & (lane == 3), summed, 0.0)
        en_out[i] = jnp.sum(mine) * (1.0 / (atoms * n_space))
    block = jnp.where(lane == 0, summed[imgs : imgs + 1, 0:1], 0.0)
    block = jnp.where(lane == 1, ff, block)
    summed = everywhere(block, part_b, send_b, recv_b, n_image, me_i, lambda p: (p, me_s))
    ratio = 0.1 * jnp.sqrt(summed[0:1, 0:1] / (summed[0:1, 1:2] + 1e-06)) + 0.1
    for i in range(imgs):
        neb = force[i] + coefs[i] * spreads[i]
        moved = 0.9 * vel[i] + ratio * neb
        new = pos[i] + 0.1 * moved
        for c in range(3):
            neb_out[c, i : i + 1, :] = neb[c : c + 1]
            vel_out[c, i : i + 1, :] = moved[c : c + 1]
            pos_out[c, i : i + 1, :] = new[c : c + 1]


def local(n_image, n_space, *args):
    pos, nbr, a1, b1 = args[0], args[4], args[7], args[8]
    imgs, _, atoms = pos.shape
    slots = nbr.shape[1]
    nb, hid = a1.shape
    ch = b1.shape[1]
    ghost = atoms // 2
    span = atoms + 2 * ghost
    edges = slots * atoms
    args = list(args)
    for j in (0, 1):
        args[j] = jnp.transpose(args[j], (1, 0, 2))
    for j in (10, 14):
        args[j] = args[j].reshape(1, -1)
    vm = pltpu.VMEM
    dma = pltpu.SemaphoreType.DMA
    scratch = [
        vm((imgs, 3, atoms), f32),
        vm((imgs, 3, atoms), f32),
        vm((imgs, span, edges), b16),
        vm((8, span), f32),
        vm((3, slots, atoms), f32),
        vm((imgs, 4, slots, atoms), f32),
        vm((imgs, 9, slots, atoms), f32),
        vm((imgs, 9, slots, atoms), f32),
        vm((imgs, slots, atoms), f32),
        vm((imgs, slots, ch, atoms), f32),
        vm((imgs, slots, ch, atoms), f32),
        vm((slots, ch, atoms), f32),
        vm((imgs, slots, hid, atoms), f32),
        vm((imgs, slots, hid, atoms), f32),
        vm((imgs, 9, ch, atoms), f32),
        vm((9, ch, atoms), f32),
        vm((imgs, ch, atoms), f32),
        vm((imgs, ch, atoms), f32),
        vm((imgs, ch, span), f32),
        vm((2 * ch, edges), b16),
        vm((8, edges), f32),
        vm((imgs, 8, span), f32),
        vm((imgs, 3, atoms), f32),
        vm((2 * hid, 4 * nb), b16),
        vm((2 * nb, 2 * hid), b16),
        vm((2 * nb, 2 * hid), b16),
        vm((ch, 3 * hid), b16),
        vm((2 * hid, 2 * ch), b16),
        vm((ch, 3 * hid), b16),
        vm((2 * hid, 2 * ch), b16),
        vm((ch, 9 * ch), b16),
        vm((6 * ch, 2 * ch), b16),
        vm((ch, 9 * ch), b16),
        vm((6 * ch, 2 * ch), b16),
        vm((2, ch, atoms), f32),
        vm((imgs, 1, 1), f32),
        vm((2, imgs, 3, ghost), f32),
        vm((2, imgs, ch, ghost), f32),
        vm((2, imgs, ch, ghost), f32),
        vm((2, imgs, 8, ghost), f32),
        vm((2, 3, atoms), f32),
        vm((n_space, 8, 128), f32),
        vm((n_image, 8, 128), f32),
        dma((4,)),
        dma((4,)),
        dma((imgs, 2)),
        dma((imgs, 2)),
        dma((imgs, 2)),
        dma((imgs, 2)),
        dma((imgs, 2)),
        dma((imgs, 2)),
        dma((n_space,)),
        dma((n_space,)),
        dma((n_image,)),
        dma((n_image,)),
    ]
    in_specs = [pl.BlockSpec(memory_space=pltpu.VMEM)] * len(args)
    in_specs[6] = pl.BlockSpec(memory_space=pltpu.SMEM)
    state = jax.ShapeDtypeStruct((3, imgs, atoms), f32)
    neb, vel, new, en = pl.pallas_call(
        functools.partial(kernel, n_image, n_space),
        out_shape=[state, state, state, jax.ShapeDtypeStruct((imgs,), f32)],
        in_specs=in_specs,
        out_specs=[pl.BlockSpec(memory_space=pltpu.VMEM)] * 3
        + [pl.BlockSpec(memory_space=pltpu.SMEM)],
        scratch_shapes=scratch,
        compiler_params=pltpu.CompilerParams(
            collective_id=0, has_side_effects=True, vmem_limit_bytes=56 * 1024 * 1024
        ),
    )(*args)
    neb, vel, new = [jnp.transpose(x, (1, 0, 2)) for x in (neb, vel, new)]
    return neb, vel, new, en


def solution(mesh):
    state = P("image", None, "space")
    end = P(None, "space")
    in_specs = (state, state, end, end, state, P("image", "space")) + (P(),) * 9
    out_specs = (state, state, state, P("image"))
    body = functools.partial(local, mesh.shape["image"], mesh.shape["space"])
    return jax.shard_map(body, mesh=mesh, in_specs=in_specs, out_specs=out_specs, check_vma=False)
```

```python
import functools
import math

import jax
import jax.numpy as jnp
from jax import lax
from jax.experimental import pallas as pl
from jax.experimental.pallas import tpu as pltpu
from jax.sharding import PartitionSpec as P

f32 = jnp.float32
b16 = jnp.bfloat16
ROOT3 = math.sqrt(3.0)


def nn(a, b):
    return lax.dot_general(a, b, (((1,), (0,)), ((), ())), preferred_element_type=f32)


def nt(a, b):
    return lax.dot_general(a, b, (((1,), (1,)), ((), ())), preferred_element_type=f32)


def pieces(x):
    high = x.astype(b16).astype(f32)
    return high, x - high


def rows(*parts):
    return jnp.concatenate(parts, axis=0).astype(b16)


def eye(size):
    r = lax.broadcasted_iota(jnp.int32, (size, size), 0)
    c = lax.broadcasted_iota(jnp.int32, (size, size), 1)
    return jnp.where(r == c, 1.0, 0.0).astype(b16)


def total(x):
    return jnp.sum(jnp.sum(x, axis=1, keepdims=True), axis=0, keepdims=True)


def kernel(
    n_image,
    n_space,
    pos_in,
    vel_in,
    first_end,
    last_end,
    nbr,
    cnt,
    climb,
    a1,
    b1,
    m1,
    q1,
    a2,
    b2,
    m2,
    q2,
    neb_out,
    vel_out,
    pos_out,
    en_out,
    pos,
    vel,
    hot,
    ext,
    nbp,
    geo,
    ang,
    dang,
    dlen,
    rad1,
    rad2,
    feat_nb,
    slope1,
    slope2,
    mom1,
    mom2,
    oslope1,
    feat,
    gfeat,
    dq,
    drow,
    gpos,
    force,
    wa_f,
    wa_b1,
    wa_b2,
    wb_f1,
    wb_b1,
    wb_f2,
    wb_b2,
    wm_f1,
    wm_b1,
    wm_f2,
    wm_b2,
    rcol,
    energy,
    ghost_pos,
    ghost_feat,
    ghost_grad,
    ghost_force,
    side_img,
    part_a,
    part_b,
    send_edge,
    recv_edge,
    send_feat,
    recv_feat,
    send_grad,
    recv_grad,
    send_force,
    recv_force,
    send_a,
    recv_a,
    send_b,
    recv_b,
):
    _, imgs, atoms = pos_in.shape
    ghost = atoms // 2
    span = atoms + 2 * ghost
    slots = nbr.shape[1]
    hid = a1.shape[1]
    nb = a1.shape[0]
    ch = b1.shape[1]
    me_i = lax.axis_index("image")
    me_s = lax.axis_index("space")
    low = lax.rem(me_s + n_space - 1, n_space)
    upp = lax.rem(me_s + 1, n_space)
    prv = lax.rem(me_i + n_image - 1, n_image)
    nxt = lax.rem(me_i + 1, n_image)
    mesh_id = pl.DeviceIdType.MESH

    def remote(src, dst, ss, rs, dev):
        return pltpu.make_async_remote_copy(
            src_ref=src, dst_ref=dst, send_sem=ss, recv_sem=rs, device_id=dev, device_id_type=mesh_id
        )

    barrier = pltpu.get_barrier_semaphore()
    for off in range(1, n_space):
        pl.semaphore_signal(
            barrier, inc=1, device_id=(me_i, lax.rem(me_s + off, n_space)), device_id_type=mesh_id
        )
    for off in range(1, n_image):
        pl.semaphore_signal(
            barrier, inc=1, device_id=(lax.rem(me_i + off, n_image), me_s), device_id_type=mesh_id
        )

    for i in range(imgs):
        for c in range(3):
            pos[i, c : c + 1, :] = pos_in[c, i : i + 1, :]
            vel[i, c : c + 1, :] = vel_in[c, i : i + 1, :]

    place = lax.broadcasted_iota(jnp.int32, (span, atoms), 0)

    def lanes(k):
        return pl.ds(pl.multiple_of(k * atoms, atoms), atoms)

    for i in range(imgs):

        def build(k, carry, i=i):
            idx = nbr[i, pl.ds(k, 1), :]
            idx = jnp.where(cnt[i : i + 1, :] > k, idx, -1)
            hot[i, :, lanes(k)] = jnp.where(place == idx, 1.0, 0.0).astype(b16)
            return carry

        if i == 0:
            lax.fori_loop(0, slots, build, 0)
            pl.semaphore_wait(barrier, n_space - 1 + n_image - 1)
            edge = [
                remote(
                    pos.at[:, :, pl.ds(0, ghost)],
                    ghost_pos.at[1],
                    send_edge.at[0],
                    recv_edge.at[0],
                    (me_i, low),
                ),
                remote(
                    pos.at[:, :, pl.ds(atoms - ghost, ghost)],
                    ghost_pos.at[0],
                    send_edge.at[1],
                    recv_edge.at[1],
                    (me_i, upp),
                ),
                remote(
                    pos.at[0], side_img.at[1], send_edge.at[2], recv_edge.at[2], (prv, me_s)
                ),
                remote(
                    pos.at[imgs - 1], side_img.at[0], send_edge.at[3], recv_edge.at[3], (nxt, me_s)
                ),
            ]
            for c in edge:
                c.start()
        else:
            lax.fori_loop(0, slots, build, 0)

    fwd_a = []
    for a, wab in ((a1, wa_b1), (a2, wa_b2)):
        hi, lo = pieces(a[...])
        fwd_a.append(nt(eye(hid), rows(hi, hi, lo, lo)))
        both = jnp.concatenate([hi, lo], axis=0)
        wab[...] = jnp.concatenate([both, both], axis=1).astype(b16)
    wa_f[...] = rows(*fwd_a)
    unit = eye(ch)
    for b, wbf, wbb in ((b1, wb_f1, wb_b1), (b2, wb_f2, wb_b2)):
        hi, lo = pieces(b[...])
        wbf[...] = nt(unit, rows(hi, hi, lo)).astype(b16)
        both = jnp.concatenate([hi, lo], axis=0)
        wbb[...] = jnp.concatenate([both, both], axis=1).astype(b16)
    for m, wmf, wmb in ((m1, wm_f1, wm_b1), (m2, wm_f2, wm_b2)):
        hi, lo = pieces(m[...])
        wmf[...] = nt(unit, rows(hi, hi, lo)).astype(b16)
        both = jnp.concatenate([hi, lo], axis=0)
        wmb[...] = jnp.concatenate([both, both], axis=1).astype(b16)
    for j, q in enumerate((q1, q2)):
        wide = jnp.broadcast_to(q[...], (atoms, ch))
        hi, rest = pieces(wide)
        mid, lo = pieces(rest)
        rcol[j] = nt(unit, hi.astype(b16)) + nt(unit, mid.astype(b16)) + nt(unit, lo.astype(b16))

    group = math.gcd(slots, 8)
    pair = 2 if slots % 2 == 0 else 1
    centre = 0.5 * lax.broadcasted_iota(jnp.int32, (nb, group * atoms), 0).astype(f32)

    def wide(parts):
        return jnp.concatenate(parts, axis=1)

    cstep = 32
    lt = 128

    def moments(i, rad, scale_by, mom):
        def block(cb, carry):
            cs = pl.ds(pl.multiple_of(cb * cstep, cstep), cstep)
            for t in range(atoms // lt):
                ls = pl.ds(t * lt, lt)
                acc = [None] * 9
                for k in range(slots):
                    r = rad[i, k, cs, ls]
                    if scale_by is not None:
                        r = r * scale_by[k, cs, ls]
                    for l in range(9):
                        term = r if l == 0 else r * ang[i, l, k : k + 1, ls]
                        acc[l] = term if k == 0 else acc[l] + term
                for l in range(9):
                    mom[l, cs, ls] = acc[l] * (1.0 / slots)
            return carry

        lax.fori_loop(0, ch // cstep, block, 0)

    def mixed(mom, wmf):
        inv0 = mom[0]
        inv1 = mom[1] * mom[1] + mom[2] * mom[2] + mom[3] * mom[3]
        inv2 = (
            mom[4] * mom[4]
            + mom[5] * mom[5]
            + mom[6] * mom[6]
            + mom[7] * mom[7]
            + mom[8] * mom[8]
        )
        h0, l0 = pieces(inv0)
        h1, l1 = pieces(inv1)
        h2, l2 = pieces(inv2)
        pre = nn(wmf[...], rows(h0, h1, h2, l0, l1, l2, h0, h1, h2))
        sig = 0.5 + 0.5 * jnp.tanh(0.5 * pre)
        return pre * sig, sig * (1.0 + pre * (1.0 - sig))

    def unmixed(mom, wmb, dpre):
        hi, lo = pieces(dpre)
        both = nn(wmb[...], rows(hi, lo))
        dinv = (both[: 3 * ch] + both[3 * ch :]) * (1.0 / slots)
        mom[0] = dinv[:ch]
        d1 = 2.0 * dinv[ch : 2 * ch]
        d2 = 2.0 * dinv[2 * ch :]
        for l in range(1, 9):
            mom[l] = mom[l] * (d1 if l < 4 else d2)

    def radial_back(i, drad, wbb, wab, slope, add):
        def step(s, carry):
            ks = [s * group + j for j in range(group)]
            hi, lo = pieces(wide([drad[i, k] for k in ks]))
            both = nn(wbb[...], rows(hi, lo))
            dz = (both[:hid] + both[hid:]) * wide([slope[i, k] for k in ks])
            zh, zl = pieces(dz)
            db = nn(wab[...], rows(zh, zl))
            gap = wide([geo[i, 3, pl.ds(k, 1), :] for k in ks]) - centre
            db = (db[:nb] + db[nb:]) * jnp.exp(-2.0 * gap * gap) * (-4.0 * gap)
            dd = jnp.sum(db, axis=0, keepdims=True)
            if add:
                dd = dd + wide([dlen[i, pl.ds(k, 1), :] for k in ks])
            for j, k in enumerate(ks):
                dlen[i, pl.ds(k, 1), :] = dd[:, j * atoms : (j + 1) * atoms]
            return carry

        lax.fori_loop(0, slots // group, step, 0)

    def phase_one(i):
        ext[...] = jnp.zeros_like(ext)
        ext[0:3, pl.ds(0, ghost)] = ghost_pos[0, i]
        ext[0:3, pl.ds(ghost, atoms)] = pos[i]
        ext[0:3, pl.ds(ghost + atoms, ghost)] = ghost_pos[1, i]
        hi, rest = pieces(ext[...])
        mid, lo = pieces(rest)
        three = rows(hi, mid, lo, jnp.zeros_like(lo))

        got = nn(three, hot[i])
        got = got[0:8] + got[8:16] + got[16:24]
        for k in range(slots):
            for c in range(3):
                nbp[c, k : k + 1, :] = got[c : c + 1, k * atoms : (k + 1) * atoms]
        r = [nbp[c] - pos[i, c : c + 1, :] for c in range(3)]
        sq = r[0] * r[0] + r[1] * r[1] + r[2] * r[2] + 1.0
        length = jnp.sqrt(sq)
        inverse = 1.0 / length
        ux, uy, uz = r[0] * inverse, r[1] * inverse, r[2] * inverse
        geo[i, 0], geo[i, 1], geo[i, 2], geo[i, 3] = ux, uy, uz, length
        ang[i, 1], ang[i, 2], ang[i, 3] = ux, uy, uz
        ang[i, 4] = ux * uy
        ang[i, 5] = uy * uz
        ang[i, 6] = ux * uz
        ang[i, 7] = 0.5 * (ux * ux - uy * uy)
        ang[i, 8] = (3.0 * uz * uz - 1.0) / (2.0 * ROOT3)

        def radial(s, carry):
            ks = [s * group + j for j in range(group)]
            gap = wide([geo[i, 3, pl.ds(k, 1), :] for k in ks]) - centre
            hi, lo = pieces(jnp.exp(-2.0 * gap * gap))
            z = nn(wa_f[...], rows(hi, lo, hi, lo))
            sig = 0.5 + 0.5 * jnp.tanh(0.5 * z)
            h = z * sig
            slope = sig * (1.0 + z * (1.0 - sig))
            hh, hl = pieces(h)
            alive = wide([jnp.where(cnt[i : i + 1, :] > k, 1.0, 0.0) for k in ks])
            r1 = nn(wb_f1[...], rows(hh[:hid], hl[:hid], hh[:hid])) * alive
            r2 = nn(wb_f2[...], rows(hh[hid:], hl[hid:], hh[hid:]))
            for j, k in enumerate(ks):
                at = slice(j * atoms, (j + 1) * atoms)
                slope1[i, k] = slope[:hid, at]
                slope2[i, k] = slope[hid:, at]
                rad1[i, k] = r1[:, at]
                rad2[i, k] = r2[:, at]
            return carry

        lax.fori_loop(0, slots // group, radial, 0)
        moments(i, rad1, None, mom1.at[i])
        out, slope = mixed(mom1.at[i], wm_f1)
        oslope1[i] = slope
        feat[i] = out
        energy[i] = total(out * rcol[0])

    def phase_two(i):
        whole = jnp.concatenate([ghost_feat[0, i], feat[i], ghost_feat[1, i]], axis=1)
        two = rows(*pieces(whole))

        def pick(s, carry):
            cols = pl.ds(pl.multiple_of(s * group * atoms, group * atoms), group * atoms)
            got = nn(two, hot[i, :, cols])
            got = got[:ch] + got[ch:]
            for j in range(group):
                feat_nb[s * group + j] = got[:, j * atoms : (j + 1) * atoms]
            return carry

        lax.fori_loop(0, slots // group, pick, 0)
        moments(i, rad2, feat_nb, mom2)
        out, slope = mixed(mom2, wm_f2)
        energy[i] = energy[i] + total(out * rcol[1])
        unmixed(mom2, wm_b2, rcol[1] * slope)

        def back(s, carry):
            ks = [s * pair + j for j in range(pair)]
            row = [[None] + [ang[i, l, pl.ds(k, 1), :] for l in range(1, 9)] for k in ks]
            sums = [[] for k in ks]
            for t in range(atoms // lt):
                ls = pl.ds(t * lt, lt)
                ys = [
                    [None] + [jnp.broadcast_to(r[:, t * lt : (t + 1) * lt], (8, lt)) for r in w[1:]]
                    for w in row
                ]
                dy = [[None] * 9 for k in ks]
                for c in range(ch // 8):
                    cs = pl.ds(c * 8, 8)
                    raw = [rad2[i, k, cs, ls] for k in ks]
                    q = [feat_nb[k, cs, ls] for k in ks]
                    full = [x * y for x, y in zip(raw, q)]
                    drf = [mom2[0, cs, ls]] * pair
                    for l in range(1, 9):
                        g = mom2[l, cs, ls]
                        for j in range(pair):
                            drf[j] = drf[j] + g * ys[j][l]
                            term = g * full[j]
                            dy[j][l] = term if c == 0 else dy[j][l] + term
                    for j, k in enumerate(ks):
                        rad2[i, k, cs, ls] = drf[j] * q[j]
                        feat_nb[k, cs, ls] = drf[j] * raw[j]
                for j in range(pair):
                    sums[j].append([jnp.sum(x, axis=0, keepdims=True) for x in dy[j][1:]])
            for j, k in enumerate(ks):
                for l in range(1, 9):
                    dang[i, l, pl.ds(k, 1), :] = wide([x[l - 1] for x in sums[j]])
                dq[:, lanes(k)] = rows(*pieces(feat_nb[k]))
            return carry

        lax.fori_loop(0, slots // pair, back, 0)
        both = nt(dq[...], hot[i])
        gfeat[i] = both[:ch] + both[ch:]

    def phase_two_rest(i):
        radial_back(i, rad2, wb_b2, wa_b2, slope2, False)

    def phase_three(i):
        own = gfeat[i, :, pl.ds(ghost, atoms)]
        back_in = jnp.concatenate([ghost_grad[0, i], ghost_grad[1, i]], axis=1)
        unmixed(mom1.at[i], wm_b1, (own + back_in + rcol[0]) * oslope1[i])

        def back(s, carry):
            ks = [s * pair + j for j in range(pair)]
            row = [[None] + [ang[i, l, pl.ds(k, 1), :] for l in range(1, 9)] for k in ks]
            old = [[None] + [dang[i, l, pl.ds(k, 1), :] for l in range(1, 9)] for k in ks]
            sums = [[] for k in ks]
            for t in range(atoms // lt):
                ls = pl.ds(t * lt, lt)
                ys = [
                    [None] + [jnp.broadcast_to(r[:, t * lt : (t + 1) * lt], (8, lt)) for r in w[1:]]
                    for w in row
                ]
                alive = [
                    jnp.broadcast_to(jnp.where(cnt[i : i + 1, ls] > k, 1.0, 0.0), (8, lt)) for k in ks
                ]
                dy = [[None] * 9 for k in ks]
                for c in range(ch // 8):
                    cs = pl.ds(c * 8, 8)
                    full = [rad1[i, k, cs, ls] for k in ks]
                    drf = [mom1[i, 0, cs, ls]] * pair
                    for l in range(1, 9):
                        g = mom1[i, l, cs, ls]
                        for j in range(pair):
                            drf[j] = drf[j] + g * ys[j][l]
                            term = g * full[j]
                            dy[j][l] = term if c == 0 else dy[j][l] + term
                    for j, k in enumerate(ks):
                        rad1[i, k, cs, ls] = drf[j] * alive[j]
                for j in range(pair):
                    sums[j].append([jnp.sum(x, axis=0, keepdims=True) for x in dy[j][1:]])
            for j, k in enumerate(ks):
                for l in range(1, 9):
                    dang[i, l, pl.ds(k, 1), :] = old[j][l] + wide([x[l - 1] for x in sums[j]])
            return carry

        lax.fori_loop(0, slots // pair, back, 0)
        radial_back(i, rad1, wb_b1, wa_b1, slope1, True)
        ux, uy, uz, length = geo[i, 0], geo[i, 1], geo[i, 2], geo[i, 3]
        inverse = 1.0 / length
        y = [None] + [dang[i, l] for l in range(1, 9)]
        du = [
            y[1] + uy * y[4] + uz * y[6] + ux * y[7],
            y[2] + ux * y[4] + uz * y[5] - uy * y[7],
            y[3] + uy * y[5] + ux * y[6] + ROOT3 * uz * y[8],
        ]
        lean = dlen[i] - (du[0] * ux + du[1] * uy + du[2] * uz) * inverse
        drow[...] = jnp.zeros_like(drow)
        for c, u in enumerate((ux, uy, uz)):
            dr = du[c] * inverse + u * lean
            for k in range(slots):
                drow[c : c + 1, k * atoms : (k + 1) * atoms] = dr[k : k + 1]
            force[i, c : c + 1, :] = jnp.sum(dr, axis=0, keepdims=True)
        both = nt(rows(*pieces(drow[...])), hot[i])
        gpos[i] = both[:8] + both[8:]

    def swap(i, src, head, tail, dst_upper, dst_lower, ss, rs):
        both = [
            remote(src.at[i, :, head], dst_upper.at[i], ss.at[i, 0], rs.at[i, 0], (me_i, low)),
            remote(src.at[i, :, tail], dst_lower.at[i], ss.at[i, 1], rs.at[i, 1], (me_i, upp)),
        ]
        for c in both:
            c.start()
        return both

    own_head, own_tail = pl.ds(0, ghost), pl.ds(atoms - ghost, ghost)
    ext_head, ext_tail = pl.ds(0, ghost), pl.ds(ghost + atoms, ghost)
    for c in edge:
        c.wait()
    sent = []
    for i in range(imgs):
        phase_one(i)
        sent.append(
            swap(
                i, feat, own_head, own_tail, ghost_feat.at[1], ghost_feat.at[0], send_feat, recv_feat
            )
        )
    back_sent = []
    for i in range(imgs):
        for c in sent[i]:
            c.wait()
        phase_two(i)
        back_sent.append(
            swap(
                i, gfeat, ext_head, ext_tail, ghost_grad.at[1], ghost_grad.at[0], send_grad, recv_grad
            )
        )
        phase_two_rest(i)
    force_sent = []
    for i in range(imgs):
        for c in back_sent[i]:
            c.wait()
        phase_three(i)
        force_sent.append(
            swap(
                i, gpos, ext_head, ext_tail, ghost_force.at[1], ghost_force.at[0], send_force, recv_force
            )
        )

    lane = lax.broadcasted_iota(jnp.int32, (8, 128), 1)
    line = lax.broadcasted_iota(jnp.int32, (8, 128), 0)
    spreads = []
    vv = jnp.zeros((1, 1), f32)
    block = jnp.zeros((8, 128), f32)
    for i in range(imgs):
        here = pos[i]
        if i == 0:
            before = jnp.where(me_i == 0, first_end[...], side_img[0])
        else:
            before = pos[i - 1]
        if i == imgs - 1:
            after = jnp.where(me_i == n_image - 1, last_end[...], side_img[1])
        else:
            after = pos[i + 1]
        spread = after - before
        spreads.append(spread)
        ahead = after - here
        behind = here - before
        vv = vv + total(vel[i] * vel[i])
        for c in force_sent[i]:
            c.wait()
        back_in = jnp.concatenate([ghost_force[0, i], ghost_force[1, i]], axis=1)
        f = force[i] - gpos[i, 0:3, pl.ds(ghost, atoms)] - back_in[0:3]
        force[i] = f
        values = (
            total(ahead * ahead),
            total(behind * behind),
            total(spread * spread),
            energy[i],
            total(f * spread),
            total(f * f),
        )
        for j, v in enumerate(values):
            block = jnp.where((line == i) & (lane == j), v, block)
    block = jnp.where((line == imgs) & (lane == 0), vv, block)

    def everywhere(block, part, ss, rs, count, mine, device):
        part[mine] = block
        out = []
        for off in range(1, count):
            peer = lax.rem(mine + off, count)
            c = remote(part.at[mine], part.at[mine], ss.at[off], rs.at[mine], device(peer))
            c.start()
            out.append(c)
        for off in range(1, count):
            peer = lax.rem(mine + off, count)
            remote(
                part.at[mine], part.at[peer], ss.at[off], rs.at[peer], device(peer)
            ).wait_recv()
        for c in out:
            c.wait_send()
        summed = part[0]
        for j in range(1, count):
            summed = summed + part[j]
        return summed

    summed = everywhere(block, part_a, send_a, recv_a, n_space, me_s, lambda p: (me_i, p))
    coefs = []
    ff = jnp.zeros((1, 1), f32)
    for i in range(imgs):
        sa, sb, st, fd, fs = [summed[i : i + 1, j : j + 1] for j in (0, 1, 2, 4, 5)]
        norm = jnp.sqrt(st + 1e-06)
        along = fd / norm
        spring = 5.0 * (jnp.sqrt(sa) - jnp.sqrt(sb))
        climbing = jnp.where(me_i * imgs + i == climb[0], 1.0, 0.0)
        coef = (-(1.0 + climbing) * along + (1.0 - climbing) * spring) / norm
        coefs.append(coef)
        ff = ff + jnp.maximum(fs + 2.0 * coef * fd + coef * coef * st, 0.0)
        mine = jnp.where((line == i) & (lane == 3), summed, 0.0)
        en_out[i] = jnp.sum(mine) * (1.0 / (atoms * n_space))
    block = jnp.where(lane == 0, summed[imgs : imgs + 1, 0:1], 0.0)
    block = jnp.where(lane == 1, ff, block)
    summed = everywhere(block, part_b, send_b, recv_b, n_image, me_i, lambda p: (p, me_s))
    ratio = 0.1 * jnp.sqrt(summed[0:1, 0:1] / (summed[0:1, 1:2] + 1e-06)) + 0.1
    for i in range(imgs):
        neb = force[i] + coefs[i] * spreads[i]
        moved = 0.9 * vel[i] + ratio * neb
        new = pos[i] + 0.1 * moved
        for c in range(3):
            neb_out[c, i : i + 1, :] = neb[c : c + 1]
            vel_out[c, i : i + 1, :] = moved[c : c + 1]
            pos_out[c, i : i + 1, :] = new[c : c + 1]


def local(n_image, n_space, *args):
    pos, nbr, a1, b1 = args[0], args[4], args[7], args[8]
    imgs, _, atoms = pos.shape
    slots = nbr.shape[1]
    nb, hid = a1.shape
    ch = b1.shape[1]
    ghost = atoms // 2
    span = atoms + 2 * ghost
    edges = slots * atoms
    args = list(args)
    for j in (0, 1):
        args[j] = jnp.transpose(args[j], (1, 0, 2))
    for j in (10, 14):
        args[j] = args[j].reshape(1, -1)
    vm = pltpu.VMEM
    dma = pltpu.SemaphoreType.DMA
    scratch = [
        vm((imgs, 3, atoms), f32),
        vm((imgs, 3, atoms), f32),
        vm((imgs, span, edges), b16),
        vm((8, span), f32),
        vm((3, slots, atoms), f32),
        vm((imgs, 4, slots, atoms), f32),
        vm((imgs, 9, slots, atoms), f32),
        vm((imgs, 9, slots, atoms), f32),
        vm((imgs, slots, atoms), f32),
        vm((imgs, slots, ch, atoms), f32),
        vm((imgs, slots, ch, atoms), f32),
        vm((slots, ch, atoms), f32),
        vm((imgs, slots, hid, atoms), f32),
        vm((imgs, slots, hid, atoms), f32),
        vm((imgs, 9, ch, atoms), f32),
        vm((9, ch, atoms), f32),
        vm((imgs, ch, atoms), f32),
        vm((imgs, ch, atoms), f32),
        vm((imgs, ch, span), f32),
        vm((2 * ch, edges), b16),
        vm((8, edges), f32),
        vm((imgs, 8, span), f32),
        vm((imgs, 3, atoms), f32),
        vm((2 * hid, 4 * nb), b16),
        vm((2 * nb, 2 * hid), b16),
        vm((2 * nb, 2 * hid), b16),
        vm((ch, 3 * hid), b16),
        vm((2 * hid, 2 * ch), b16),
        vm((ch, 3 * hid), b16),
        vm((2 * hid, 2 * ch), b16),
        vm((ch, 9 * ch), b16),
        vm((6 * ch, 2 * ch), b16),
        vm((ch, 9 * ch), b16),
        vm((6 * ch, 2 * ch), b16),
        vm((2, ch, atoms), f32),
        vm((imgs, 1, 1), f32),
        vm((2, imgs, 3, ghost), f32),
        vm((2, imgs, ch, ghost), f32),
        vm((2, imgs, ch, ghost), f32),
        vm((2, imgs, 8, ghost), f32),
        vm((2, 3, atoms), f32),
        vm((n_space, 8, 128), f32),
        vm((n_image, 8, 128), f32),
        dma((4,)),
        dma((4,)),
        dma((imgs, 2)),
        dma((imgs, 2)),
        dma((imgs, 2)),
        dma((imgs, 2)),
        dma((imgs, 2)),
        dma((imgs, 2)),
        dma((n_space,)),
        dma((n_space,)),
        dma((n_image,)),
        dma((n_image,)),
    ]
    in_specs = [pl.BlockSpec(memory_space=pltpu.VMEM)] * len(args)
    in_specs[6] = pl.BlockSpec(memory_space=pltpu.SMEM)
    state = jax.ShapeDtypeStruct((3, imgs, atoms), f32)
    neb, vel, new, en = pl.pallas_call(
        functools.partial(kernel, n_image, n_space),
        out_shape=[state, state, state, jax.ShapeDtypeStruct((imgs,), f32)],
        in_specs=in_specs,
        out_specs=[pl.BlockSpec(memory_space=pltpu.VMEM)] * 3
        + [pl.BlockSpec(memory_space=pltpu.SMEM)],
        scratch_shapes=scratch,
        compiler_params=pltpu.CompilerParams(
            collective_id=0, has_side_effects=True, vmem_limit_bytes=56 * 1024 * 1024
        ),
    )(*args)
    neb, vel, new = [jnp.transpose(x, (1, 0, 2)) for x in (neb, vel, new)]
    return neb, vel, new, en


def solution(mesh):
    state = P("image", None, "space")
    end = P(None, "space")
    in_specs = (state, state, end, end, state, P("image", "space")) + (P(),) * 9
    out_specs = (state, state, state, P("image"))
    body = functools.partial(local, mesh.shape["image"], mesh.shape["space"])
    return jax.shard_map(body, mesh=mesh, in_specs=in_specs, out_specs=out_specs, check_vma=False)
```
